512 devices in a mesh: src: 64 (over x, y_hi, z), tgt: 8 (over y_lo, core).
Axes of the slice: x: 4, y: 8 (y_hi: 2, y_lo: 4; y = y_hi * 4 + y_lo), z: 8, core: 2. Of those that a mesh axis runs over, the one named last changes fastest.
Arguments:
- source_points: float32 [32, 16384], P(None, 'src'), may hold values from -1.5 to 1.5
- source_potential: float32 [16384], P('src'), may hold values from 2 to 4
- source_cotangent: float32 [16384], P('src'), may hold values from -25 to 25
- target_points: float32 [32, 32768], P(None, 'tgt'), may hold values from -1.5 to 1.5
- target_potential: float32 [32768], P('tgt'), may hold values from 2 to 4
- target_cotangent: float32 [32768], P('tgt'), may hold values from -25 to 25
Outputs:
- source_adjoint: float32 [16384], P('src')
- target_adjoint: float32 [32768], P('tgt')
- source_gradient: float32 [32, 16384], P(None, 'src')
- target_gradient: float32 [32, 32768], P(None, 'tgt')
The draws below stay inside these ranges and needn't reach their ends.
All inputs are finite; a program needn't handle non-finite values.
Results may differ from the reference program's by a relative error of at most 0.0003.
Values sent between devices are 32-bit elements; how exact they have to be, the bound alone decides.
A program may use at most 64 MiB of HBM per device.

```python
import math
import jax
import jax.numpy as jnp
from jax import lax

D = 32
ITERS = 2
NS = 16384
NT = 32768


def rising_scale(scale_key, item_count, growth):
    position = jnp.arange(item_count).astype(jnp.float32) / max(item_count - 1, 1)
    spread = jnp.exp(jax.random.uniform(scale_key, (item_count,), jnp.float32) * math.log(10.0))
    return 0.15 * spread * jnp.exp(position * math.log(growth))


def draw_source_cotangent(key, part):
    key = jax.random.fold_in(key, 11)
    noise_key, scale_key = jax.random.split(key)
    noise = jnp.clip(jax.random.normal(noise_key, (NS,), jnp.float32), -4.0, 4.0)
    return rising_scale(scale_key, NS, 3.0) * noise


def draw_target_cotangent(key, part):
    key = jax.random.fold_in(key, 23)
    noise_key, scale_key = jax.random.split(key)
    noise = jnp.clip(jax.random.normal(noise_key, (NT,), jnp.float32), -4.0, 4.0)
    return rising_scale(scale_key, NT, 3.0) * noise


def levels(key, shape, cuts, least, top_value):
    def one(axis_at, shards_of):
        heights = jax.random.uniform(jax.random.fold_in(jax.random.fold_in(key, 6), axis_at), (shards_of,), jnp.float32, least / len(cuts), top_value / len(cuts))
        return jnp.repeat(jnp.exp(heights), shape[axis_at] // shards_of).reshape((-1,) + (1,) * (len(shape) - axis_at - 1))

    loudness = one(*cuts[0])
    for cut in cuts[1:]:
        loudness = loudness * one(*cut)
    return loudness


def bell_draw(key, extent, width, limit, pieces=(), kind=jnp.bfloat16):
    array = jax.random.normal(key, extent, jnp.float32) * width
    if len(pieces) > 0:
        array = levels(key, extent, pieces, -0.22, 0.18) * array
    return jnp.clip(array, min=-limit, max=limit).astype(kind)


def setup_inputs(seed: int = 0) -> dict:
    streams_of = jax.random.split(jax.random.key(seed), 7)
    return {
        "source_points": bell_draw(streams_of[0], (D, NS), 0.25, 1.5, ((1, 64),), jnp.float32),
        "source_potential": jnp.clip(2.0 + 2.0 * jax.random.uniform(streams_of[1], (NS,), jnp.float32) ** levels(streams_of[1], (NS,), ((0, 64),), -0.2, 0.2), 2.0, 4.0),
        "source_cotangent": draw_source_cotangent(jax.random.fold_in(streams_of[6], 71), 0),
        "target_points": bell_draw(streams_of[3], (D, NT), 0.25, 1.5, ((1, 8),), jnp.float32),
        "target_potential": jnp.clip(2.0 + 2.0 * jax.random.uniform(streams_of[4], (NT,), jnp.float32) ** levels(streams_of[4], (NT,), ((0, 8),), -0.2, 0.2), 2.0, 4.0),
        "target_cotangent": draw_target_cotangent(jax.random.fold_in(streams_of[6], 71), 0),
    }


epsilon = 0.5
ridge = 0.5
highest = lax.Precision.HIGHEST

def transport_tile(source_block, norm_block, potential_block, target_points, target_norms, target_potential, factor):
    cross_terms = lax.dot_general(source_block, target_points, (((0,), (0,)), ((), ())), precision=highest, preferred_element_type=jnp.float32)
    distance = norm_block[:, None] + target_norms[None, :] - 2.0 * cross_terms
    return jnp.exp(potential_block[:, None] + target_potential[None, :] - distance / epsilon) * factor

def sweep_blocks(source_points, source_potential, target_points, target_potential, visit, initial):
    source_total = source_points.shape[1]
    target_total = target_points.shape[1]
    factor = 1.0 / math.sqrt(source_total * target_total)
    block_width = math.gcd(source_total, 1024)
    block_total = source_total // block_width
    source_norms = lax.optimization_barrier(jnp.sum(source_points * source_points, axis=0))
    target_norms = lax.optimization_barrier(jnp.sum(target_points * target_points, axis=0))

    def advance(totals, block_id):
        offset = block_id * block_width
        source_block = lax.dynamic_slice_in_dim(source_points, offset, block_width, 1)
        norm_block = lax.dynamic_slice_in_dim(source_norms, offset, block_width, 0)
        potential_block = lax.dynamic_slice_in_dim(source_potential, offset, block_width, 0)
        transport = transport_tile(source_block, norm_block, potential_block, target_points, target_norms, target_potential, factor)
        return visit(totals, transport, source_block, offset, block_width)
    return lax.scan(advance, initial, jnp.arange(block_total, dtype=jnp.int32))

def apply_transport(source_points, source_potential, target_points, target_potential, source_vectors, target_vectors):

    def visit(column_total, transport, source_block, offset, block_width):
        vector_block = lax.dynamic_slice_in_dim(source_vectors, offset, block_width, 1)
        row_part = lax.dot_general(target_vectors, transport, (((1,), (1,)), ((), ())), precision=highest, preferred_element_type=jnp.float32)
        column_total = column_total + jnp.dot(vector_block, transport, precision=highest, preferred_element_type=jnp.float32)
        return (column_total, row_part)
    initial = jnp.zeros((source_vectors.shape[0], target_points.shape[1]), jnp.float32)
    column_total, row_parts = sweep_blocks(source_points, source_potential, target_points, target_potential, visit, initial)
    row_total = jnp.transpose(row_parts, (1, 0, 2)).reshape(target_vectors.shape[0], source_points.shape[1])
    return (row_total, column_total)

def reference(source_points, source_potential, source_cotangent, target_points, target_potential, target_cotangent):

    def operator(search_source, search_target, margins):
        if margins is None:
            source_vectors = jnp.stack([jnp.ones_like(search_source), search_source])
            target_vectors = jnp.stack([jnp.ones_like(search_target), search_target])
        else:
            source_vectors = search_source[None, :]
            target_vectors = search_target[None, :]
        row_total, column_total = apply_transport(source_points, source_potential, target_points, target_potential, source_vectors, target_vectors)
        if margins is None:
            margins = (row_total[0], column_total[0])
        image_source = (margins[0] + ridge) * search_source + row_total[-1]
        image_target = (margins[1] + ridge) * search_target + column_total[-1]
        return (image_source, image_target, margins)
    adjoint_source = jnp.zeros_like(source_cotangent)
    adjoint_target = jnp.zeros_like(target_cotangent)
    residual_source, residual_target = (source_cotangent, target_cotangent)
    direction_source, direction_target = (source_cotangent, target_cotangent)
    norm_now = jnp.sum(residual_source * residual_source) + jnp.sum(residual_target * residual_target)
    margins = None
    for iteration in range(ITERS):
        image_source, image_target, margins = operator(direction_source, direction_target, margins)
        curve_value = jnp.sum(direction_source * image_source) + jnp.sum(direction_target * image_target)
        step_size = norm_now / curve_value
        adjoint_source = adjoint_source + step_size * direction_source
        adjoint_target = adjoint_target + step_size * direction_target
        residual_source = residual_source - step_size * image_source
        residual_target = residual_target - step_size * image_target
        if iteration + 1 < ITERS:
            norm_next = jnp.sum(residual_source * residual_source) + jnp.sum(residual_target * residual_target)
            direction_ratio = norm_next / norm_now
            direction_source = residual_source + direction_ratio * direction_source
            direction_target = residual_target + direction_ratio * direction_target
            norm_now = norm_next

    def visit(totals, transport, source_block, offset, block_width):
        column_weight, column_points = totals
        adjoint_block = lax.dynamic_slice_in_dim(adjoint_source, offset, block_width, 0)
        weight = transport * (adjoint_block[:, None] + adjoint_target[None, :])
        row_weight = lax.optimization_barrier(jnp.sum(weight, axis=1))
        row_points = lax.dot_general(target_points, weight, (((1,), (1,)), ((), ())), precision=highest, preferred_element_type=jnp.float32)
        source_grad = 2.0 / epsilon * (row_weight[None, :] * source_block - row_points)
        column_weight = column_weight + lax.optimization_barrier(jnp.sum(weight, axis=0))
        column_points = column_points + jnp.dot(source_block, weight, precision=highest, preferred_element_type=jnp.float32)
        return ((column_weight, column_points), source_grad)
    initial = (jnp.zeros((target_points.shape[1],), jnp.float32), jnp.zeros(target_points.shape, jnp.float32))
    totals, grad_parts = sweep_blocks(source_points, source_potential, target_points, target_potential, visit, initial)
    source_gradient = jnp.transpose(grad_parts, (1, 0, 2)).reshape(source_points.shape)
    target_gradient = 2.0 / epsilon * (totals[0][None, :] * target_points - totals[1])
    return (adjoint_source, adjoint_target, source_gradient, target_gradient)
```

```python
import functools
import math

import jax
import jax.numpy as jnp
from jax import lax
from jax.experimental import pallas as pl
from jax.experimental.pallas import tpu as pltpu
from jax.sharding import PartitionSpec as P

MESH = pl.DeviceIdType.MESH
F32 = jnp.float32
BF16 = jnp.bfloat16

NX, NY, NZ, NTG = 4, 2, 8, 8
NYZ = NY * NZ

D = 32
ROWS = 256
COLS = 4096
CHUNK = 512
RIDGE = 0.5
LOG2E = 1.4426950408889634
EXTRA = 512


def split2(v):
    high = v.astype(BF16)
    return high, (v - high.astype(F32)).astype(BF16)


def split3(v):
    high = v.astype(BF16)
    rest = v - high.astype(F32)
    mid = rest.astype(BF16)
    return high, mid, (rest - mid.astype(F32)).astype(BF16)


def dot_nn(a, b):
    return lax.dot_general(a, b, (((1,), (0,)), ((), ())), preferred_element_type=F32)


def dot_nt(a, b):
    return lax.dot_general(a, b, (((1,), (1,)), ((), ())), preferred_element_type=F32)


def dot_tn(a, b):
    return lax.dot_general(a, b, (((0,), (0,)), ((), ())), preferred_element_type=F32)


def kernel(
    factor_log2,
    xs_ref, xpot_ref, xcot_ref, ys_ref, ypot_ref, ycot_ref,
    sadj_ref, tadj_ref, sgrad_ref, tgrad_ref,
    bk, ph, pl_, colcrit, work, ubuf, wbuf,
    t1s, t1r, a1s, a1r, a1m, a1q, a2s, a2r, a2m, a2q,
    gc, gv, rxc, rxv, hc, hv, ryc, ryv,
    t2s, t2r, t3s, t3r, ag,
    send, recv,
):
    src = lax.axis_index("src")
    tgt = lax.axis_index("tgt")
    x = src // NYZ
    y = (src // NZ) % NY
    z = src % NZ

    def at(dx=0, dy=0, dz=0, dt=0):
        there = ((x + dx) % NX) * NYZ + ((y + dy) % NY) * NZ + (z + dz) % NZ
        return (there, (tgt + dt) % NTG)

    def post(source, target, sem, peer):
        pltpu.make_async_remote_copy(
            src_ref=source, dst_ref=target, send_sem=send.at[sem], recv_sem=recv.at[sem],
            device_id=peer, device_id_type=MESH,
        ).start()

    def arrive(ref, sem):
        pltpu.make_async_copy(ref, ref, recv.at[sem]).wait()

    z_peers = [dict(dz=k) for k in range(1, NZ)]
    xy_peers = [dict(dx=k // NY, dy=k % NY) for k in range(1, NX * NY)]
    yz_peers = [dict(dy=k // NZ, dz=k % NZ) for k in range(1, NYZ)]
    x_peers = [dict(dx=k) for k in range(1, NX)]
    t_peers = [dict(dt=k) for k in range(1, NTG)]

    barrier = pltpu.get_barrier_semaphore()
    greet = t_peers + yz_peers + [p for p in xy_peers if p["dx"]]
    for p in greet:
        pl.semaphore_signal(barrier, inc=1, device_id=at(**p), device_id_type=MESH)

    xs = xs_ref[...]
    cs = xcot_ref[...]
    ct = ycot_ref[...]
    x1, x2, x3 = split3(xs * (4.0 * LOG2E))
    row_term = (xpot_ref[...] - 2.0 * jnp.sum(xs * xs, axis=0, keepdims=True)) * LOG2E
    r1, r2, r3 = split3(row_term)
    one_r = jnp.ones((1, ROWS), F32)
    tail_a = jnp.concatenate(
        [r1.astype(F32), r2.astype(F32), r3.astype(F32), one_r, one_r, one_r,
         jnp.zeros((26, ROWS), F32)], axis=0,
    ).astype(BF16)
    ak = jnp.concatenate([x1, x1, x2, x2, x1, x3, tail_a], axis=0)

    ones_crit = jnp.ones((1, ROWS), F32)
    cs_h, cs_l = split2(cs)
    s_crit = jnp.concatenate(
        [ones_crit, cs_h.astype(F32), cs_l.astype(F32), jnp.zeros((13, ROWS), F32)], axis=0
    ).astype(BF16)

    def build(i, row_acc):
        at_c = pl.ds(pl.multiple_of(i * CHUNK, CHUNK), CHUNK)
        yc = ys_ref[:, at_c]
        y1, y2, y3 = split3(yc)
        col_term = (ypot_ref[:, at_c] - 2.0 * jnp.sum(yc * yc, axis=0, keepdims=True)) * LOG2E
        c1, c2, c3 = split3(col_term + factor_log2)
        one_c = jnp.ones((1, CHUNK), F32)
        tail_b = jnp.concatenate(
            [one_c, one_c, one_c, c1.astype(F32), c2.astype(F32), c3.astype(F32),
             jnp.zeros((26, CHUNK), F32)], axis=0,
        ).astype(BF16)
        bk[...] = jnp.concatenate([y1, y2, y1, y2, y3, y1, tail_b], axis=0)
        plan = jnp.exp2(dot_tn(ak, bk[...]))
        high, low = split2(plan)
        ph[:, at_c] = high
        pl_[:, at_c] = low
        colcrit[:, at_c] = dot_nn(s_crit, high) + dot_nn(s_crit, low)
        ct_h, ct_l = split2(ct_at(at_c))
        t_crit = jnp.concatenate(
            [one_c, ct_h.astype(F32), ct_l.astype(F32), jnp.zeros((13, CHUNK), F32)], axis=0
        ).astype(BF16)
        return row_acc + dot_nt(t_crit, high) + dot_nt(t_crit, low)

    def ct_at(at_c):
        return ycot_ref[:, at_c]

    row_crit = lax.fori_loop(0, COLS // CHUNK, build, jnp.zeros((16, ROWS), F32))
    rm_part = row_crit[0:1]
    pct_part = row_crit[1:2] + row_crit[2:3]
    cm_part = colcrit[0:1, :]
    pcs_part = colcrit[1:2, :] + colcrit[2:3, :]

    pl.semaphore_wait(barrier, len(greet))

    t1s[...] = jnp.concatenate([rm_part, pct_part], axis=1)
    a1s[...] = cm_part * ct + pcs_part
    for i, p in enumerate(t_peers):
        post(t1s, t1r.at[i], 0, at(**p))
    for i, p in enumerate(z_peers):
        post(a1s, a1r.at[i], 1, at(**p))

    def col_products(vectors, width):
        high, low = split2(vectors)
        stack = jnp.concatenate([high, low], axis=0)

        def step(i, c):
            at_c = pl.ds(pl.multiple_of(i * CHUNK, CHUNK), CHUNK)
            r = dot_nn(stack, ph[:, at_c]) + dot_nn(stack, pl_[:, at_c])
            work[0:width, at_c] = r[:width] + r[width:]
            return c

        lax.fori_loop(0, COLS // CHUNK, step, 0)

    def row_products(make, width):
        def step(i, acc):
            at_c = pl.ds(pl.multiple_of(i * CHUNK, CHUNK), CHUNK)
            high, low = split2(make(at_c))
            stack = jnp.concatenate([high, low], axis=0)
            r = dot_nt(stack, ph[:, at_c]) + dot_nt(stack, pl_[:, at_c])
            return acc + r[:width] + r[width:]

        return lax.fori_loop(0, COLS // CHUNK, step, jnp.zeros((width, ROWS), F32))

    def place(o):
        ox, oy, oz = o // NYZ, (o // NZ) % NY, o % NZ
        return ((ox - x + NX) % NX) * NYZ + ((oy - y + NY) % NY) * NZ + (oz - z + NZ) % NZ

    col_products(jnp.concatenate([xs, xs * cs], axis=0), 64)
    for c in range(COLS // 128):
        lanes = slice(c * 128, c * 128 + 128)
        yc = ys_ref[:, lanes]
        u = colcrit[0:1, lanes] * yc - work[0:32, lanes]
        ubuf[:, lanes] = u
        g = ycot_ref[:, lanes] * u + pcs_part[:, lanes] * yc - work[32:64, lanes]
        gc[place(2 * c)] = g[0:16]
        gc[place(2 * c + 1)] = g[16:32]

    arrive(t1r, 0)
    rows_sum = t1s[...]
    for i in range(NTG - 1):
        rows_sum = rows_sum + t1r[i]
    rm = rows_sum[:, :ROWS]
    vs = rm * cs + rows_sum[:, ROWS:]
    col_products(jnp.concatenate([xs * vs, vs, jnp.zeros((15, ROWS), F32)], axis=0), 48)
    pvs_part = work[32:33, :]
    a2s[...] = jnp.concatenate(
        [
            jnp.concatenate([pvs_part, cs * cs, cs * vs], axis=1),
            jnp.concatenate([cm_part, vs * vs, rm * vs * vs], axis=1),
        ],
        axis=0,
    )

    arrive(a1r, 1)
    total = a1s[...]
    for i in range(NZ - 1):
        total = total + a1r[i]
    a1m[...] = total
    for i, p in enumerate(xy_peers):
        post(a1m, a1q.at[i], 2, at(**p))
    for i, p in enumerate(z_peers):
        post(a2s, a2r.at[i], 3, at(**p))

    def post_x(buf, into, base):
        for g in (3, 2, 1, 0):
            for m in range(1, NX):
                post(buf.at[pl.ds(m * NYZ + 4 * g, 4)], into.at[g, m - 1], base + g, at(dx=m))

    post_x(gc, rxc, 8)

    for c in range(COLS // 128):
        lanes = slice(c * 128, c * 128 + 128)
        wbuf[:, lanes] = work[32:33, lanes] * ys_ref[:, lanes] - work[0:32, lanes]

    def make_c(at_c):
        yc = ys_ref[:, at_c]
        return jnp.concatenate([yc, yc * ct_at(at_c)], axis=0)

    rp = row_products(make_c, 64)
    row_u = rm_part * xs - rp[0:32]
    t2s[0] = cs * row_u + pct_part * xs - rp[32:64]
    for i, p in enumerate(t_peers):
        post(t2s.at[0], t2r.at[0, i], 4, at(**p))

    arrive(a2r, 3)
    total2 = a2s[...]
    for i in range(NZ - 1):
        total2 = total2 + a2r[i]
    a2m[...] = total2
    for i, p in enumerate(xy_peers):
        post(a2m, a2q.at[i], 5, at(**p))

    arrive(a1q, 2)
    vt = a1m[...]
    for i in range(NX * NY - 1):
        vt = vt + a1q[i]
    for c in range(COLS // 128):
        lanes = slice(c * 128, c * 128 + 128)
        g = vt[:, lanes] * ubuf[:, lanes] + wbuf[:, lanes]
        gv[place(2 * c)] = g[0:16]
        gv[place(2 * c + 1)] = g[16:32]
    post_x(gv, rxv, 12)
    tadj_ref[...] = vt

    def make_v(at_c):
        v = tadj_ref[:, at_c]
        return jnp.concatenate([ys_ref[:, at_c] * v, v, jnp.zeros((15, CHUNK), F32)], axis=0)

    rp = row_products(make_v, 48)
    t2s[1] = vs * row_u + rp[32:33] * xs - rp[0:32]
    for i, p in enumerate(t_peers):
        post(t2s.at[1], t2r.at[1, i], 6, at(**p))

    def add_x(buf, inbox, held, outbox, base, sem):
        for g in (3, 2, 1, 0):
            arrive(inbox.at[g], base + g)
            for s in range(4 * g, 4 * g + 4):
                held[s] = buf[s] + inbox[g, 0, s - 4 * g] + inbox[g, 1, s - 4 * g] + inbox[g, 2, s - 4 * g]
            for s in range(4 * g, 4 * g + 4):
                if s:
                    post(held.at[s], outbox.at[s - 1], sem, at(dy=s // NZ, dz=s % NZ))

    add_x(gc, rxc, hc, ryc, 8, 16)
    add_x(gv, rxv, hv, ryv, 12, 17)

    arrive(a2q, 5)
    total2 = a2m[...]
    for i in range(NX * NY - 1):
        total2 = total2 + a2q[i]
    pvs = total2[0:1, :COLS]
    cm = total2[1:2, :COLS]
    over_src = [
        total2[0:1, COLS : COLS + 256],
        total2[0:1, COLS + 256 :],
        total2[1:2, COLS : COLS + 256],
        total2[1:2, COLS + 256 :],
    ]

    def fold(v):
        acc = v[:, 0:128]
        for c in range(1, COLS // 128):
            acc = acc + v[:, c * 128 : c * 128 + 128]
        return acc

    t3s[...] = jnp.concatenate(
        [fold(ct * ct), fold(ct * vt), fold(vt * vt), fold(vt * (cm * vt + 2.0 * pvs))], axis=1
    )
    for i, p in enumerate(t_peers):
        post(t3s, t3r.at[i], 7, at(**p))
    arrive(t3r, 7)
    over_tgt = t3s[...]
    for i in range(NTG - 1):
        over_tgt = over_tgt + t3r[i]
    m0, g1, g2, g3 = (
        jnp.sum(a[:, 0:128] + a[:, 128:256] + over_tgt[:, q * 128 : q * 128 + 128], axis=1, keepdims=True)
        for q, a in enumerate(over_src)
    )
    mu = g1 / m0
    h2 = jnp.maximum(g2 - g1 * mu, 0.0)
    h3 = g3 - 2.0 * mu * g2 + mu * mu * g1
    step0 = 1.0 / (RIDGE + mu)
    below = RIDGE * h2 + h3 - step0 * h2 * h2 / m0
    step1 = h2 / jnp.maximum(jnp.maximum(below, RIDGE * h2), 1e-37)
    beta = step0 * step0 * h2 / m0
    of_c = step0 + step1 * (beta + step0 * mu)
    of_v = -(step0 * step1)

    sadj_ref[...] = of_c * cs + of_v * vs
    tadj_ref[...] = of_c * ct + of_v * vt
    k_c = 4.0 * of_c
    k_v = 4.0 * of_v

    arrive(ryc, 16)
    piece_c = hc[0]
    for s in range(NYZ - 1):
        piece_c = piece_c + ryc[s]
    arrive(ryv, 17)
    piece_v = hv[0]
    for s in range(NYZ - 1):
        piece_v = piece_v + ryv[s]
    ag[0, 0] = k_c * piece_c + k_v * piece_v
    for s in range(NYZ - 1, 0, -1):
        post(ag.at[0, 0], ag.at[0, s], 18 + s // 4, at(dy=s // NZ, dz=s % NZ))

    arrive(t2r.at[0], 4)
    arrive(t2r.at[1], 6)
    grad_c, grad_v = t2s[0], t2s[1]
    for i in range(NTG - 1):
        grad_c = grad_c + t2r[0, i]
        grad_v = grad_v + t2r[1, i]
    sgrad_ref[...] = k_c * grad_c + k_v * grad_v

    for g in range(4):
        arrive(ag.at[0, pl.ds(max(4 * g, 1), 4 if g else 3)], 18 + g)
        for m in range(1, NX):
            post(ag.at[0, pl.ds(4 * g, 4)], ag.at[m, pl.ds(4 * g, 4)], 22, at(dx=m))
    arrive(ag.at[pl.ds(1, 3)], 22)

    for c in range(COLS // 128):
        for h in range(2):
            o = 2 * c + h
            ox, oy, oz = o // NYZ, (o // NZ) % NY, o % NZ
            slot = ((y - oy + NY) % NY) * NZ + (z - oz + NZ) % NZ
            tgrad_ref[16 * h : 16 * h + 16, c * 128 : c * 128 + 128] = ag[(x - ox + NX) % NX, slot]

    def sent(ref, sem):
        pltpu.make_async_copy(ref, ref, send.at[sem]).wait()

    sent(t1r, 0)
    sent(a1r, 1)
    sent(a1q, 2)
    sent(a2r, 3)
    sent(t2r.at[0], 4)
    sent(a2q, 5)
    sent(t2r.at[1], 6)
    sent(t3r, 7)
    for g in range(4):
        sent(rxc.at[g], 8 + g)
        sent(rxv.at[g], 12 + g)
        sent(ag.at[0, pl.ds(max(4 * g, 1), 4 if g else 3)], 18 + g)
    sent(ryc, 16)
    sent(ryv, 17)
    sent(ag.at[pl.ds(1, 3)], 22)


def solution(mesh):
    def local(xs, xpot, xcot, ys, ypot, ycot):
        count = xs.shape[1] * mesh.shape["src"] * ys.shape[1] * mesh.shape["tgt"]
        vmem = pl.BlockSpec(memory_space=pltpu.VMEM)
        sadj, tadj, sgrad, tgrad = pl.pallas_call(
            functools.partial(kernel, -0.5 * math.log2(count)),
            out_shape=(
                jax.ShapeDtypeStruct((1, ROWS), F32),
                jax.ShapeDtypeStruct((1, COLS), F32),
                jax.ShapeDtypeStruct((D, ROWS), F32),
                jax.ShapeDtypeStruct((D, COLS), F32),
            ),
            in_specs=[vmem] * 6,
            out_specs=(vmem,) * 4,
            scratch_shapes=[
                pltpu.VMEM((224, CHUNK), BF16),
                pltpu.VMEM((ROWS, COLS), BF16),
                pltpu.VMEM((ROWS, COLS), BF16),
                pltpu.VMEM((16, COLS), F32),
                pltpu.VMEM((64, COLS), F32),
                pltpu.VMEM((D, COLS), F32),
                pltpu.VMEM((D, COLS), F32),
                pltpu.VMEM((1, 2 * ROWS), F32),
                pltpu.VMEM((NTG - 1, 1, 2 * ROWS), F32),
                pltpu.VMEM((1, COLS), F32),
                pltpu.VMEM((NZ - 1, 1, COLS), F32),
                pltpu.VMEM((1, COLS), F32),
                pltpu.VMEM((NX * NY - 1, 1, COLS), F32),
                pltpu.VMEM((2, COLS + EXTRA), F32),
                pltpu.VMEM((NZ - 1, 2, COLS + EXTRA), F32),
                pltpu.VMEM((2, COLS + EXTRA), F32),
                pltpu.VMEM((NX * NY - 1, 2, COLS + EXTRA), F32),
                pltpu.VMEM((NX * NYZ, 16, 128), F32),
                pltpu.VMEM((NX * NYZ, 16, 128), F32),
                pltpu.VMEM((4, NX - 1, 4, 16, 128), F32),
                pltpu.VMEM((4, NX - 1, 4, 16, 128), F32),
                pltpu.VMEM((NYZ, 16, 128), F32),
                pltpu.VMEM((NYZ, 16, 128), F32),
                pltpu.VMEM((NYZ - 1, 16, 128), F32),
                pltpu.VMEM((NYZ - 1, 16, 128), F32),
                pltpu.VMEM((2, D, ROWS), F32),
                pltpu.VMEM((2, NTG - 1, D, ROWS), F32),
                pltpu.VMEM((1, 512), F32),
                pltpu.VMEM((NTG - 1, 1, 512), F32),
                pltpu.VMEM((NX, NYZ, 16, 128), F32),
                pltpu.SemaphoreType.DMA((23,)),
                pltpu.SemaphoreType.DMA((23,)),
            ],
            compiler_params=pltpu.CompilerParams(
                collective_id=0, has_side_effects=True, vmem_limit_bytes=48 * 2**20
            ),
        )(xs, xpot.reshape(1, ROWS), xcot.reshape(1, ROWS), ys, ypot.reshape(1, COLS), ycot.reshape(1, COLS))
        return sadj.reshape(ROWS), tadj.reshape(COLS), sgrad, tgrad

    return jax.shard_map(
        local,
        mesh=mesh,
        in_specs=(P(None, "src"), P("src"), P("src"), P(None, "tgt"), P("tgt"), P("tgt")),
        out_specs=(P("src"), P("tgt"), P(None, "src"), P(None, "tgt")),
        check_vma=False,
    )
```

```python
import functools
import math

import jax
import jax.numpy as jnp
from jax import lax
from jax.experimental import pallas as pl
from jax.experimental.pallas import tpu as pltpu
from jax.sharding import PartitionSpec as P

MESH = pl.DeviceIdType.MESH
F32 = jnp.float32
BF16 = jnp.bfloat16

NX, NY, NZ, NTG = 4, 2, 8, 8
NYZ = NY * NZ

D = 32
ROWS = 256
COLS = 4096
CHUNK = 512
RIDGE = 0.5
LOG2E = 1.4426950408889634


def split2(v):
    high = v.astype(BF16)
    return high, (v - high.astype(F32)).astype(BF16)


def split3(v):
    high = v.astype(BF16)
    rest = v - high.astype(F32)
    mid = rest.astype(BF16)
    return high, mid, (rest - mid.astype(F32)).astype(BF16)


def dot_nn(a, b):
    return lax.dot_general(a, b, (((1,), (0,)), ((), ())), preferred_element_type=F32)


def dot_nt(a, b):
    return lax.dot_general(a, b, (((1,), (1,)), ((), ())), preferred_element_type=F32)


def dot_tn(a, b):
    return lax.dot_general(a, b, (((0,), (0,)), ((), ())), preferred_element_type=F32)


def kernel(
    factor_log2,
    xs_hbm, xpot_hbm, xcot_hbm, ys_hbm, ypot_hbm, ycot_hbm,
    sadj_hbm, tadj_hbm, sgrad_hbm, tgrad_hbm,
    xs_ref, xpot_ref, xcot_ref, ys_ref, ypot_ref, ycot_ref,
    sadj_ref, tadj_ref, sgrad_ref, tgrad_ref,
    bk, ph, pl_, cm_ref, pcs_ref, work, ubuf, wbuf,
    t1s, t1r, a1s, a1r, a1m, a1q,
    gc, gv, rxc, rxv, hc, hv, ryc, ryv,
    t2s, t2r, t4, qs, qr, qm, qq, ag,
    load, store, send, recv,
):
    loads = [
        pltpu.make_async_copy(a, b, load.at[i])
        for i, (a, b) in enumerate(
            [(xs_hbm, xs_ref), (xpot_hbm, xpot_ref), (xcot_hbm, xcot_ref),
             (ypot_hbm, ypot_ref), (ycot_hbm, ycot_ref)]
            + [(ys_hbm.at[:, pl.ds(k * 1024, 1024)], ys_ref.at[:, pl.ds(k * 1024, 1024)]) for k in range(4)]
        )
    ]
    for c in loads:
        c.start()
    src = lax.axis_index("src")
    tgt = lax.axis_index("tgt")
    x = src // NYZ
    y = (src // NZ) % NY
    z = src % NZ

    def at(dx=0, dy=0, dz=0, dt=0):
        there = ((x + dx) % NX) * NYZ + ((y + dy) % NY) * NZ + (z + dz) % NZ
        return (there, (tgt + dt) % NTG)

    def post(source, target, sem, peer):
        pltpu.make_async_remote_copy(
            src_ref=source, dst_ref=target, send_sem=send.at[sem], recv_sem=recv.at[sem],
            device_id=peer, device_id_type=MESH,
        ).start()

    def arrive(ref, sem):
        pltpu.make_async_copy(ref, ref, recv.at[sem]).wait()

    z_peers = [dict(dz=k) for k in range(1, NZ)]
    xy_peers = [dict(dx=k // NY, dy=k % NY) for k in range(1, NX * NY)]
    yz_peers = [dict(dy=k // NZ, dz=k % NZ) for k in range(1, NYZ)]
    x_peers = [dict(dx=k) for k in range(1, NX)]
    t_peers = [dict(dt=k) for k in range(1, NTG)]
    tx_peers = [dict(dx=k // NTG, dt=k % NTG) for k in range(1, NX * NTG)]

    barrier = pltpu.get_barrier_semaphore()
    greet = tx_peers + yz_peers + [p for p in xy_peers if p["dx"] and p["dy"]]
    for p in greet:
        pl.semaphore_signal(barrier, inc=1, device_id=at(**p), device_id_type=MESH)

    for c in loads[:5]:
        c.wait()
    xs = xs_ref[...]
    cs = xcot_ref[...]
    ct = ycot_ref[...]
    x1, x2, x3 = split3(xs * (4.0 * LOG2E))
    row_term = (xpot_ref[...] - 2.0 * jnp.sum(xs * xs, axis=0, keepdims=True)) * LOG2E
    r1, r2, r3 = split3(row_term)
    one_r = jnp.ones((1, ROWS), F32)
    tail_a = jnp.concatenate(
        [r1.astype(F32), r2.astype(F32), r3.astype(F32), one_r, one_r, one_r,
         jnp.zeros((26, ROWS), F32)], axis=0,
    ).astype(BF16)
    ak = jnp.concatenate([x1, x1, x2, x2, x1, x3, tail_a], axis=0)

    ones_crit = jnp.ones((1, ROWS), F32)
    cs_h, cs_l = split2(cs)
    s_crit = jnp.concatenate(
        [ones_crit, cs_h.astype(F32), cs_l.astype(F32), jnp.zeros((13, ROWS), F32)], axis=0
    ).astype(BF16)

    row_crit = jnp.zeros((16, ROWS), F32)
    one_c = jnp.ones((1, CHUNK), F32)
    for i in range(COLS // CHUNK):
        if i * CHUNK % 1024 == 0:
            loads[5 + i * CHUNK // 1024].wait()
        at_c = slice(i * CHUNK, i * CHUNK + CHUNK)
        yc = ys_ref[:, at_c]
        ctc = ycot_ref[:, at_c]
        y1, y2, y3 = split3(yc)
        col_term = (ypot_ref[:, at_c] - 2.0 * jnp.sum(yc * yc, axis=0, keepdims=True)) * LOG2E
        c1, c2, c3 = split3(col_term + factor_log2)
        tail_b = jnp.concatenate(
            [one_c, one_c, one_c, c1.astype(F32), c2.astype(F32), c3.astype(F32),
             jnp.zeros((26, CHUNK), F32)], axis=0,
        ).astype(BF16)
        bk[i % 2] = jnp.concatenate([y1, y2, y1, y2, y3, y1, tail_b], axis=0)
        plan = jnp.exp2(dot_tn(ak, bk[i % 2]))
        high, low = split2(plan)
        ph[:, at_c] = high
        pl_[:, at_c] = low
        r = dot_nn(s_crit, high) + dot_nn(s_crit, low)
        cm_c = r[0:1]
        pcs_c = r[1:2] + r[2:3]
        cm_ref[:, at_c] = cm_c
        pcs_ref[:, at_c] = pcs_c
        a1s[:, at_c] = cm_c * ctc + pcs_c
        ct_h, ct_l = split2(ctc)
        t_crit = jnp.concatenate(
            [one_c, ct_h.astype(F32), ct_l.astype(F32), jnp.zeros((13, CHUNK), F32)], axis=0
        ).astype(BF16)
        row_crit = row_crit + dot_nt(t_crit, high) + dot_nt(t_crit, low)

    rm_part = row_crit[0:1]
    pct_part = row_crit[1:2] + row_crit[2:3]
    t1s[...] = jnp.concatenate([rm_part, pct_part], axis=1)

    pl.semaphore_wait(barrier, len(greet))

    for i, p in enumerate(t_peers):
        post(t1s, t1r.at[i], 0, at(**p))
    for i, p in enumerate(z_peers):
        post(a1s, a1r.at[i], 1, at(**p))

    def col_products(vectors, width):
        high, low = split2(vectors)
        stack = jnp.concatenate([high, low], axis=0)

        def step(i, c):
            at_c = pl.ds(pl.multiple_of(i * CHUNK, CHUNK), CHUNK)
            r = dot_nn(stack, ph[:, at_c]) + dot_nn(stack, pl_[:, at_c])
            work[0:width, at_c] = r[:width] + r[width:]
            return c

        lax.fori_loop(0, COLS // CHUNK, step, 0)

    def row_products(make, width):
        def step(i, acc):
            at_c = pl.ds(pl.multiple_of(i * CHUNK, CHUNK), CHUNK)
            high, low = split2(make(at_c))
            stack = jnp.concatenate([high, low], axis=0)
            r = dot_nt(stack, ph[:, at_c]) + dot_nt(stack, pl_[:, at_c])
            return acc + r[:width] + r[width:]

        return lax.fori_loop(0, COLS // CHUNK, step, jnp.zeros((width, ROWS), F32))

    def place(o):
        ox, oy, oz = o // NYZ, (o // NZ) % NY, o % NZ
        return ((ox - x + NX) % NX) * NYZ + ((oy - y + NY) % NY) * NZ + (oz - z + NZ) % NZ

    col_products(jnp.concatenate([xs, xs * cs], axis=0), 64)
    for c in range(COLS // 128):
        lanes = slice(c * 128, c * 128 + 128)
        yc = ys_ref[:, lanes]
        u = cm_ref[:, lanes] * yc - work[0:32, lanes]
        ubuf[:, lanes] = u
        g = ycot_ref[:, lanes] * u + pcs_ref[:, lanes] * yc - work[32:64, lanes]
        gc[place(2 * c)] = g[0:16]
        gc[place(2 * c + 1)] = g[16:32]

    def post_x(buf, into, base):
        for g in (3, 2, 1, 0):
            for m in range(1, NX):
                post(buf.at[pl.ds(m * NYZ + 4 * g, 4)], into.at[g, m - 1], base + g, at(dx=m))

    post_x(gc, rxc, 8)

    arrive(t1r, 0)
    rows_sum = t1s[...]
    for i in range(NTG - 1):
        rows_sum = rows_sum + t1r[i]
    rm = rows_sum[:, :ROWS]
    vs = rm * cs + rows_sum[:, ROWS:]
    col_products(jnp.concatenate([xs * vs, vs, jnp.zeros((15, ROWS), F32)], axis=0), 48)
    for c in range(COLS // 128):
        lanes = slice(c * 128, c * 128 + 128)
        wbuf[:, lanes] = work[32:33, lanes] * ys_ref[:, lanes] - work[0:32, lanes]

    arrive(a1r, 1)
    total = a1s[...]
    for i in range(NZ - 1):
        total = total + a1r[i]
    a1m[...] = total
    for i, p in enumerate(xy_peers):
        post(a1m, a1q.at[i], 2, at(**p))

    def make_c(at_c):
        yc = ys_ref[:, at_c]
        return jnp.concatenate([yc, yc * ycot_ref[:, at_c]], axis=0)

    rp = row_products(make_c, 64)
    row_u = rm_part * xs - rp[0:32]
    row_c = cs * row_u + pct_part * xs - rp[32:64]

    def add_x(buf, inbox, held, outbox, base, sem):
        for g in (3, 2, 1, 0):
            arrive(inbox.at[g], base + g)
            for s in range(4 * g, 4 * g + 4):
                held[s] = buf[s] + inbox[g, 0, s - 4 * g] + inbox[g, 1, s - 4 * g] + inbox[g, 2, s - 4 * g]
            for s in range(4 * g, 4 * g + 4):
                if s:
                    post(held.at[s], outbox.at[s - 1], sem, at(dy=s // NZ, dz=s % NZ))

    add_x(gc, rxc, hc, ryc, 8, 16)

    arrive(a1q, 2)
    vt = a1m[...]
    for i in range(NX * NY - 1):
        vt = vt + a1q[i]
    for c in range(COLS // 128):
        lanes = slice(c * 128, c * 128 + 128)
        g = vt[:, lanes] * ubuf[:, lanes] + wbuf[:, lanes]
        gv[place(2 * c)] = g[0:16]
        gv[place(2 * c + 1)] = g[16:32]
    post_x(gv, rxv, 12)
    tadj_ref[...] = vt

    def fold(v):
        acc = v[:, 0:128]
        for c in range(1, v.shape[1] // 128):
            acc = acc + v[:, c * 128 : c * 128 + 128]
        return acc

    of_src, of_tgt = 1.0 / NTG, 1.0 / (NX * NYZ)
    ct = ycot_ref[...]
    pvs_part = work[32:33, :]
    qs[...] = jnp.concatenate(
        [
            fold(cs * cs) * of_src + fold(ct * ct) * of_tgt,
            fold(cs * vs) * of_src + fold(ct * vt) * of_tgt,
            fold(vs * vs) * of_src + fold(vt * vt) * of_tgt,
            fold(rm_part * vs * vs) + fold(vt * (cm_ref[...] * vt + 2.0 * pvs_part)),
        ],
        axis=1,
    )
    for i, p in enumerate(tx_peers):
        post(qs, qr.at[i], 3, at(**p))

    def make_v(at_c):
        v = tadj_ref[:, at_c]
        return jnp.concatenate([ys_ref[:, at_c] * v, v, jnp.zeros((15, CHUNK), F32)], axis=0)

    rp = row_products(make_v, 48)
    row_v = vs * row_u + rp[32:33] * xs - rp[0:32]
    for p in range(NTG):
        rows, lanes = slice(p // 2 * 8, p // 2 * 8 + 8), slice(p % 2 * 128, p % 2 * 128 + 128)
        slot = (p - tgt + NTG) % NTG
        t2s[slot, 0] = row_c[rows, lanes]
        t2s[slot, 1] = row_v[rows, lanes]
    for i, p in enumerate(t_peers):
        post(t2s.at[i + 1], t2r.at[i], 4, at(**p))

    add_x(gv, rxv, hv, ryv, 12, 17)

    arrive(qr, 3)
    inner = qs[...]
    for i in range(NX * NTG - 1):
        inner = inner + qr[i]
    qm[...] = inner
    for i, p in enumerate(yz_peers):
        post(qm, qq.at[i], 5, at(**p))

    arrive(ryc, 16)
    piece_c = hc[0]
    for s in range(NYZ - 1):
        piece_c = piece_c + ryc[s]
    arrive(t2r, 4)
    row_piece = t2s[0]
    for i in range(NTG - 1):
        row_piece = row_piece + t2r[i]

    arrive(qq, 5)
    inner = qm[...]
    for i in range(NYZ - 1):
        inner = inner + qq[i]
    m0, g1, g2, g3 = (
        jnp.sum(inner[:, q * 128 : q * 128 + 128], axis=1, keepdims=True) for q in range(4)
    )
    mu = g1 / m0
    h2 = jnp.maximum(g2 - g1 * mu, 0.0)
    h3 = g3 - 2.0 * mu * g2 + mu * mu * g1
    step0 = 1.0 / (RIDGE + mu)
    below = RIDGE * h2 + h3 - step0 * h2 * h2 / m0
    step1 = h2 / jnp.maximum(jnp.maximum(below, RIDGE * h2), 1e-37)
    beta = step0 * step0 * h2 / m0
    of_c = step0 + step1 * (beta + step0 * mu)
    of_v = -(step0 * step1)

    k_c = 4.0 * of_c
    k_v = 4.0 * of_v

    arrive(ryv, 17)
    piece_v = hv[0]
    for s in range(NYZ - 1):
        piece_v = piece_v + ryv[s]
    ag[0, 0] = k_c * piece_c + k_v * piece_v
    for s in range(NYZ - 1, 0, -1):
        post(ag.at[0, 0], ag.at[0, s], 18 + s // 4, at(dy=s // NZ, dz=s % NZ))

    t4[0] = k_c * row_piece[0] + k_v * row_piece[1]
    for i, p in enumerate(t_peers):
        post(t4.at[0], t4.at[i + 1], 6, at(**p))
    sadj_ref[...] = of_c * cs + of_v * vs
    tadj_ref[...] = of_c * ct + of_v * vt
    stores = [
        pltpu.make_async_copy(sadj_ref, sadj_hbm, store.at[0]),
        pltpu.make_async_copy(tadj_ref, tadj_hbm, store.at[1]),
        pltpu.make_async_copy(sgrad_ref, sgrad_hbm, store.at[2]),
    ]
    stores[0].start()
    stores[1].start()

    for g in range(4):
        arrive(ag.at[0, pl.ds(max(4 * g, 1), 4 if g else 3)], 18 + g)
        for m in range(1, NX):
            post(ag.at[0, pl.ds(4 * g, 4)], ag.at[m, pl.ds(4 * g, 4)], 22, at(dx=m))
    arrive(t4.at[pl.ds(1, NTG - 1)], 6)
    for p in range(NTG):
        rows, lanes = slice(p // 2 * 8, p // 2 * 8 + 8), slice(p % 2 * 128, p % 2 * 128 + 128)
        sgrad_ref[rows, lanes] = t4[(tgt - p + NTG) % NTG]
    stores[2].start()

    arrive(ag.at[pl.ds(1, 3)], 22)

    for c in range(COLS // 128):
        for h in range(2):
            o = 2 * c + h
            ox, oy, oz = o // NYZ, (o // NZ) % NY, o % NZ
            slot = ((y - oy + NY) % NY) * NZ + (z - oz + NZ) % NZ
            tgrad_ref[16 * h : 16 * h + 16, c * 128 : c * 128 + 128] = ag[(x - ox + NX) % NX, slot]
        if c % 8 == 7:
            lanes = pl.ds((c - 7) * 128, 1024)
            stores.append(pltpu.make_async_copy(tgrad_ref.at[:, lanes], tgrad_hbm.at[:, lanes], store.at[3 + c // 8]))
            stores[-1].start()

    def sent(ref, sem):
        pltpu.make_async_copy(ref, ref, send.at[sem]).wait()

    sent(t1r, 0)
    sent(a1r, 1)
    sent(a1q, 2)
    sent(qr, 3)
    sent(t2r, 4)
    sent(qq, 5)
    sent(t4.at[pl.ds(1, NTG - 1)], 6)
    for g in range(4):
        sent(rxc.at[g], 8 + g)
        sent(rxv.at[g], 12 + g)
        sent(ag.at[0, pl.ds(max(4 * g, 1), 4 if g else 3)], 18 + g)
    sent(ryc, 16)
    sent(ryv, 17)
    sent(ag.at[pl.ds(1, 3)], 22)
    for c in stores:
        c.wait()


def deliver(*refs):
    sources, targets, held, sem_in, sem_out = refs[:4], refs[4:8], refs[8:12], refs[12], refs[13]
    parts = [(i, slice(None)) for i in range(3)] + [(3, pl.ds(8 * k, 8)) for k in range(4)]
    fetch = [pltpu.make_async_copy(sources[i].at[r], held[i].at[r], sem_in.at[n]) for n, (i, r) in enumerate(parts)]
    store = [pltpu.make_async_copy(held[i].at[r], targets[i].at[r], sem_out.at[n]) for n, (i, r) in enumerate(parts)]
    for c in fetch:
        c.start()
    for a, b in zip(fetch, store):
        a.wait()
        b.start()
    for c in store:
        c.wait()


def solution(mesh):
    def local(xs, xpot, xcot, ys, ypot, ycot):
        count = xs.shape[1] * mesh.shape["src"] * ys.shape[1] * mesh.shape["tgt"]
        hbm = pl.BlockSpec(memory_space=pltpu.HBM)
        results = (
            jax.ShapeDtypeStruct((1, ROWS), F32),
            jax.ShapeDtypeStruct((1, COLS), F32),
            jax.ShapeDtypeStruct((D, ROWS), F32),
            jax.ShapeDtypeStruct((D, COLS), F32),
        )
        outs = pl.pallas_call(
            functools.partial(kernel, -0.5 * math.log2(count)),
            out_shape=results,
            in_specs=[hbm] * 6,
            out_specs=(hbm,) * 4,
            scratch_shapes=[
                pltpu.VMEM((D, ROWS), F32),
                pltpu.VMEM((1, ROWS), F32),
                pltpu.VMEM((1, ROWS), F32),
                pltpu.VMEM((D, COLS), F32),
                pltpu.VMEM((1, COLS), F32),
                pltpu.VMEM((1, COLS), F32),
                pltpu.VMEM((1, ROWS), F32),
                pltpu.VMEM((1, COLS), F32),
                pltpu.VMEM((D, ROWS), F32),
                pltpu.VMEM((D, COLS), F32),
                pltpu.VMEM((2, 224, CHUNK), BF16),
                pltpu.VMEM((ROWS, COLS), BF16),
                pltpu.VMEM((ROWS, COLS), BF16),
                pltpu.VMEM((1, COLS), F32),
                pltpu.VMEM((1, COLS), F32),
                pltpu.VMEM((64, COLS), F32),
                pltpu.VMEM((D, COLS), F32),
                pltpu.VMEM((D, COLS), F32),
                pltpu.VMEM((1, 2 * ROWS), F32),
                pltpu.VMEM((NTG - 1, 1, 2 * ROWS), F32),
                pltpu.VMEM((1, COLS), F32),
                pltpu.VMEM((NZ - 1, 1, COLS), F32),
                pltpu.VMEM((1, COLS), F32),
                pltpu.VMEM((NX * NY - 1, 1, COLS), F32),
                pltpu.VMEM((NX * NYZ, 16, 128), F32),
                pltpu.VMEM((NX * NYZ, 16, 128), F32),
                pltpu.VMEM((4, NX - 1, 4, 16, 128), F32),
                pltpu.VMEM((4, NX - 1, 4, 16, 128), F32),
                pltpu.VMEM((NYZ, 16, 128), F32),
                pltpu.VMEM((NYZ, 16, 128), F32),
                pltpu.VMEM((NYZ - 1, 16, 128), F32),
                pltpu.VMEM((NYZ - 1, 16, 128), F32),
                pltpu.VMEM((NTG, 2, 8, 128), F32),
                pltpu.VMEM((NTG - 1, 2, 8, 128), F32),
                pltpu.VMEM((NTG, 8, 128), F32),
                pltpu.VMEM((1, 512), F32),
                pltpu.VMEM((NX * NTG - 1, 1, 512), F32),
                pltpu.VMEM((1, 512), F32),
                pltpu.VMEM((NYZ - 1, 1, 512), F32),
                pltpu.VMEM((NX, NYZ, 16, 128), F32),
                pltpu.SemaphoreType.DMA((9,)),
                pltpu.SemaphoreType.DMA((7,)),
                pltpu.SemaphoreType.DMA((23,)),
                pltpu.SemaphoreType.DMA((23,)),
            ],
            compiler_params=pltpu.CompilerParams(
                collective_id=0, has_side_effects=True, vmem_limit_bytes=60 * 2**20
            ),
        )(xs, xpot.reshape(1, ROWS), xcot.reshape(1, ROWS), ys, ypot.reshape(1, COLS), ycot.reshape(1, COLS))
        sadj, tadj, sgrad, tgrad = pl.pallas_call(
            deliver,
            out_shape=results,
            in_specs=[hbm] * 4,
            out_specs=(hbm,) * 4,
            scratch_shapes=[pltpu.VMEM(r.shape, F32) for r in results]
            + [pltpu.SemaphoreType.DMA((7,)), pltpu.SemaphoreType.DMA((7,))],
            compiler_params=pltpu.CompilerParams(vmem_limit_bytes=60 * 2**20),
        )(*outs)
        return sadj.reshape(ROWS), tadj.reshape(COLS), sgrad, tgrad

    return jax.shard_map(
        local,
        mesh=mesh,
        in_specs=(P(None, "src"), P("src"), P("src"), P(None, "tgt"), P("tgt"), P("tgt")),
        out_specs=(P("src"), P("tgt"), P(None, "src"), P(None, "tgt")),
        check_vma=False,
    )
```

```python
import functools
import math

import jax
import jax.numpy as jnp
from jax import lax
from jax.experimental import pallas as pl
from jax.experimental.pallas import tpu as pltpu
from jax.sharding import PartitionSpec as P

MESH = pl.DeviceIdType.MESH
F32 = jnp.float32
BF16 = jnp.bfloat16

NX, NY, NZ, NTG = 4, 2, 8, 8
NYZ = NY * NZ

D = 32
ROWS = 256
COLS = 4096
CHUNK = 512
RIDGE = 0.5


def split2(v):
    high = v.astype(BF16)
    return high, (v - high.astype(F32)).astype(BF16)


def split3(v):
    high = v.astype(BF16)
    rest = v - high.astype(F32)
    mid = rest.astype(BF16)
    return high, mid, (rest - mid.astype(F32)).astype(BF16)


def dot_nn(a, b):
    return lax.dot_general(a, b, (((1,), (0,)), ((), ())), preferred_element_type=F32)


def dot_nt(a, b):
    return lax.dot_general(a, b, (((1,), (1,)), ((), ())), preferred_element_type=F32)


def dot_tn(a, b):
    return lax.dot_general(a, b, (((0,), (0,)), ((), ())), preferred_element_type=F32)


def kernel(
    factor_log,
    xs_hbm, xpot_hbm, xcot_hbm, ys_hbm, ypot_hbm, ycot_hbm,
    sadj_hbm, tadj_hbm, sgrad_hbm, tgrad_hbm,
    xs_ref, xpot_ref, xcot_ref, ys_ref, ypot_ref, ycot_ref,
    sadj_ref, tadj_ref, sgrad_ref, tgrad_ref,
    bk, ph, pl_, cm_ref, pcs_ref, work, ubuf, wbuf,
    t1s, t1r, a1s, a1r, a1m, a1q,
    gc, gv, rxc, rxv, hc, hv, ryc, ryv,
    t2s, t2r, t4, qs, qr, qm, qq, qn, qz, ag,
    load, store, send, recv,
):
    loads = [
        pltpu.make_async_copy(a, b, load.at[i])
        for i, (a, b) in enumerate(
            [(xs_hbm, xs_ref), (xpot_hbm, xpot_ref), (xcot_hbm, xcot_ref),
             (ypot_hbm, ypot_ref), (ycot_hbm, ycot_ref)]
            + [(ys_hbm.at[:, pl.ds(k * 1024, 1024)], ys_ref.at[:, pl.ds(k * 1024, 1024)]) for k in range(4)]
        )
    ]
    for c in loads:
        c.start()
    src = lax.axis_index("src")
    tgt = lax.axis_index("tgt")
    x = src // NYZ
    y = (src // NZ) % NY
    z = src % NZ

    def at(dx=0, dy=0, dz=0, dt=0):
        there = ((x + dx) % NX) * NYZ + ((y + dy) % NY) * NZ + (z + dz) % NZ
        return (there, (tgt + dt) % NTG)

    def post(source, target, sem, peer):
        pltpu.make_async_remote_copy(
            src_ref=source, dst_ref=target, send_sem=send.at[sem], recv_sem=recv.at[sem],
            device_id=peer, device_id_type=MESH,
        ).start()

    def arrive(ref, sem):
        pltpu.make_async_copy(ref, ref, recv.at[sem]).wait()

    z_peers = [dict(dz=k) for k in (4, 3, 5, 2, 6, 1, 7)]
    xy_peers = [dict(dx=k // NY, dy=k % NY) for k in (5, 3, 7, 1, 4, 2, 6)]
    yz_peers = [dict(dy=k // NZ, dz=k % NZ) for k in range(1, NYZ)]
    x_peers = [dict(dx=k) for k in range(1, NX)]
    t_peers = [dict(dt=k) for k in (4, 3, 5, 2, 6, 1, 7)]

    barrier = pltpu.get_barrier_semaphore()
    greet = yz_peers + [p for p in xy_peers if p["dx"]] + t_peers
    for p in greet:
        pl.semaphore_signal(barrier, inc=1, device_id=at(**p), device_id_type=MESH)

    for c in loads[:5]:
        c.wait()
    xs = xs_ref[...]
    cs = xcot_ref[...]
    ct = ycot_ref[...]
    x1, x2, x3 = split3(xs * 4.0)
    row_term = (xpot_ref[...] - 2.0 * jnp.sum(xs * xs, axis=0, keepdims=True))
    r1, r2, r3 = split3(row_term)
    one_r = jnp.ones((1, ROWS), F32)
    tail_a = jnp.concatenate(
        [r1.astype(F32), r2.astype(F32), r3.astype(F32), one_r, one_r, one_r,
         jnp.zeros((26, ROWS), F32)], axis=0,
    ).astype(BF16)
    ak = jnp.concatenate([x1, x1, x2, x2, x1, x3, tail_a], axis=0)

    ones_crit = jnp.ones((1, ROWS), F32)
    cs_h, cs_l = split2(cs)
    s_crit = jnp.concatenate(
        [ones_crit, cs_h.astype(F32), cs_l.astype(F32), jnp.zeros((13, ROWS), F32)], axis=0
    ).astype(BF16)

    row_crit = jnp.zeros((16, ROWS), F32)
    one_c = jnp.ones((1, CHUNK), F32)
    for i in range(COLS // CHUNK):
        if i * CHUNK % 1024 == 0:
            loads[5 + i * CHUNK // 1024].wait()
        at_c = slice(i * CHUNK, i * CHUNK + CHUNK)
        yc = ys_ref[:, at_c]
        ctc = ycot_ref[:, at_c]
        y1, y2, y3 = split3(yc)
        col_term = (ypot_ref[:, at_c] - 2.0 * jnp.sum(yc * yc, axis=0, keepdims=True))
        c1, c2, c3 = split3(col_term + factor_log)
        tail_b = jnp.concatenate(
            [one_c, one_c, one_c, c1.astype(F32), c2.astype(F32), c3.astype(F32),
             jnp.zeros((26, CHUNK), F32)], axis=0,
        ).astype(BF16)
        bk[i % 2] = jnp.concatenate([y1, y2, y1, y2, y3, y1, tail_b], axis=0)
        plan = jnp.exp(dot_tn(ak, bk[i % 2]))
        high, low = split2(plan)
        ph[:, at_c] = high
        pl_[:, at_c] = low
        r = dot_nn(s_crit, high) + dot_nn(s_crit, low)
        cm_c = r[0:1]
        pcs_c = r[1:2] + r[2:3]
        cm_ref[:, at_c] = cm_c
        pcs_ref[:, at_c] = pcs_c
        a1s[:, at_c] = cm_c * ctc + pcs_c
        ct_h, ct_l = split2(ctc)
        t_crit = jnp.concatenate(
            [one_c, ct_h.astype(F32), ct_l.astype(F32), jnp.zeros((13, CHUNK), F32)], axis=0
        ).astype(BF16)
        row_crit = row_crit + dot_nt(t_crit, high) + dot_nt(t_crit, low)

    rm_part = row_crit[0:1]
    pct_part = row_crit[1:2] + row_crit[2:3]
    t1s[...] = jnp.concatenate([rm_part, pct_part], axis=1)

    pl.semaphore_wait(barrier, len(greet))

    for i, p in enumerate(z_peers):
        post(a1s, a1r.at[i], 1, at(**p))
    for i, p in enumerate(t_peers):
        post(t1s, t1r.at[i], 0, at(**p))

    def col_products(vectors, width):
        high, low = split2(vectors)
        stack = jnp.concatenate([high, low], axis=0)

        def step(i, c):
            at_c = pl.ds(pl.multiple_of(i * CHUNK, CHUNK), CHUNK)
            r = dot_nn(stack, ph[:, at_c]) + dot_nn(stack, pl_[:, at_c])
            work[0:width, at_c] = r[:width] + r[width:]
            return c

        lax.fori_loop(0, COLS // CHUNK, step, 0)

    def row_products(make, width):
        def step(i, acc):
            at_c = pl.ds(pl.multiple_of(i * CHUNK, CHUNK), CHUNK)
            high, low = split2(make(at_c))
            stack = jnp.concatenate([high, low], axis=0)
            r = dot_nt(stack, ph[:, at_c]) + dot_nt(stack, pl_[:, at_c])
            return acc + r[:width] + r[width:]

        return lax.fori_loop(0, COLS // CHUNK, step, jnp.zeros((width, ROWS), F32))

    def place(o):
        ox, oy, oz = o // NYZ, (o // NZ) % NY, o % NZ
        return ((ox - x + NX) % NX) * NYZ + ((oy - y + NY) % NY) * NZ + (oz - z + NZ) % NZ

    col_products(jnp.concatenate([xs, xs * cs], axis=0), 64)
    for c in range(COLS // 128):
        lanes = slice(c * 128, c * 128 + 128)
        yc = ys_ref[:, lanes]
        u = cm_ref[:, lanes] * yc - work[0:32, lanes]
        ubuf[:, lanes] = u
        g = ycot_ref[:, lanes] * u + pcs_ref[:, lanes] * yc - work[32:64, lanes]
        gc[place(2 * c)] = g[0:16]
        gc[place(2 * c + 1)] = g[16:32]

    def post_x(buf, into, base):
        for g in (3, 2, 1, 0):
            for m in (2, 1, 3):
                post(buf.at[pl.ds(m * NYZ + 4 * g, 4)], into.at[g, m - 1], base + g, at(dx=m))

    post_x(gc, rxc, 8)

    arrive(t1r, 0)
    rows_sum = t1s[...]
    for i in range(NTG - 1):
        rows_sum = rows_sum + t1r[i]
    rm = rows_sum[:, :ROWS]
    vs = rm * cs + rows_sum[:, ROWS:]
    col_products(jnp.concatenate([xs * vs, vs, jnp.zeros((15, ROWS), F32)], axis=0), 48)
    for c in range(COLS // 128):
        lanes = slice(c * 128, c * 128 + 128)
        wbuf[:, lanes] = work[32:33, lanes] * ys_ref[:, lanes] - work[0:32, lanes]


    def fold(v):
        acc = v[:, 0:128]
        for c in range(1, v.shape[1] // 128):
            acc = acc + v[:, c * 128 : c * 128 + 128]
        return acc

    arrive(a1r, 1)
    total = a1s[...]
    for i in range(NZ - 1):
        total = total + a1r[i]
    a1m[...] = total
    for i, p in enumerate(xy_peers):
        post(a1m, a1q.at[i], 2, at(**p))


    def make_c(at_c):
        yc = ys_ref[:, at_c]
        return jnp.concatenate([yc, yc * ycot_ref[:, at_c]], axis=0)

    rp = row_products(make_c, 64)
    row_u = rm_part * xs - rp[0:32]
    row_c = cs * row_u + pct_part * xs - rp[32:64]

    def add_x(buf, inbox, held, outbox, base, sem):
        for g in (3, 2, 1, 0):
            arrive(inbox.at[g], base + g)
            for s in range(4 * g, 4 * g + 4):
                held[s] = buf[s] + inbox[g, 0, s - 4 * g] + inbox[g, 1, s - 4 * g] + inbox[g, 2, s - 4 * g]
            for s in range(4 * g, 4 * g + 4):
                if s:
                    post(held.at[s], outbox.at[s - 1], sem, at(dy=s // NZ, dz=s % NZ))

    add_x(gc, rxc, hc, ryc, 8, 16)

    arrive(a1q, 2)
    vt = a1m[...]
    for i in range(NX * NY - 1):
        vt = vt + a1q[i]
    for c in range(COLS // 128):
        lanes = slice(c * 128, c * 128 + 128)
        g = vt[:, lanes] * ubuf[:, lanes] + wbuf[:, lanes]
        gv[place(2 * c)] = g[0:16]
        gv[place(2 * c + 1)] = g[16:32]
    post_x(gv, rxv, 12)
    tadj_ref[...] = vt

    of_src, of_tgt = 1.0 / NTG, 1.0 / (NX * NYZ)
    ct = ycot_ref[...]
    qs[...] = jnp.concatenate(
        [
            fold(cs * cs) * of_src + fold(ct * ct) * of_tgt,
            fold(cs * vs) * of_src + fold(ct * vt) * of_tgt,
            fold(vs * vs) * of_src + fold(vt * vt) * of_tgt,
            fold(rm_part * vs * vs) + fold(vt * (cm_ref[...] * vt + 2.0 * work[32:33, :])),
        ],
        axis=1,
    )
    for i, p in enumerate(t_peers):
        post(qs, qr.at[i], 7, at(**p))

    def make_v(at_c):
        v = tadj_ref[:, at_c]
        return jnp.concatenate([ys_ref[:, at_c] * v, v, jnp.zeros((15, CHUNK), F32)], axis=0)

    rp = row_products(make_v, 48)
    row_v = vs * row_u + rp[32:33] * xs - rp[0:32]
    for p in range(NTG):
        rows, lanes = slice(p // 2 * 8, p // 2 * 8 + 8), slice(p % 2 * 128, p % 2 * 128 + 128)
        slot = (p - tgt + NTG) % NTG
        t2s[slot, 0] = row_c[rows, lanes]
        t2s[slot, 1] = row_v[rows, lanes]
    for i, p in enumerate(t_peers):
        post(t2s.at[p["dt"]], t2r.at[i], 4, at(**p))

    arrive(qr, 7)
    inner = qs[...]
    for i in range(NTG - 1):
        inner = inner + qr[i]
    qm[...] = inner
    for i, p in enumerate(xy_peers):
        post(qm, qq.at[i], 23, at(**p))

    add_x(gv, rxv, hv, ryv, 12, 17)

    arrive(qq, 23)
    inner = qm[...]
    for i in range(NX * NY - 1):
        inner = inner + qq[i]
    qn[...] = inner
    for i, p in enumerate(z_peers):
        post(qn, qz.at[i], 3, at(**p))

    arrive(ryc, 16)
    piece_c = hc[0]
    for s in range(NYZ - 1):
        piece_c = piece_c + ryc[s]
    arrive(t2r, 4)
    row_piece = t2s[0]
    for i in range(NTG - 1):
        row_piece = row_piece + t2r[i]

    arrive(qz, 3)
    inner = qn[...]
    for i in range(NZ - 1):
        inner = inner + qz[i]
    m0, g1, g2, g3 = (
        jnp.sum(inner[:, q * 128 : q * 128 + 128], axis=1, keepdims=True) for q in range(4)
    )
    mu = g1 / m0
    h2 = jnp.maximum(g2 - g1 * mu, 0.0)
    h3 = g3 - 2.0 * mu * g2 + mu * mu * g1
    step0 = 1.0 / (RIDGE + mu)
    below = RIDGE * h2 + h3 - step0 * h2 * h2 / m0
    step1 = h2 / jnp.maximum(jnp.maximum(below, RIDGE * h2), 1e-37)
    beta = step0 * step0 * h2 / m0
    of_c = step0 + step1 * (beta + step0 * mu)
    of_v = -(step0 * step1)

    k_c = 4.0 * of_c
    k_v = 4.0 * of_v

    arrive(ryv, 17)
    piece_v = hv[0]
    for s in range(NYZ - 1):
        piece_v = piece_v + ryv[s]
    ag[0, 0] = k_c * piece_c + k_v * piece_v
    for s in (12, 11, 13, 10, 14, 9, 15, 8, 4, 3, 5, 2, 6, 1, 7):
        post(ag.at[0, 0], ag.at[0, s], 18 + s // 4, at(dy=s // NZ, dz=s % NZ))

    t4[0] = k_c * row_piece[0] + k_v * row_piece[1]
    for i, p in enumerate(t_peers):
        post(t4.at[0], t4.at[p["dt"]], 6, at(**p))
    sadj_ref[...] = of_c * cs + of_v * vs
    tadj_ref[...] = of_c * ct + of_v * vt
    stores = [
        pltpu.make_async_copy(sadj_ref, sadj_hbm, store.at[0]),
        pltpu.make_async_copy(tadj_ref, tadj_hbm, store.at[1]),
        pltpu.make_async_copy(sgrad_ref, sgrad_hbm, store.at[2]),
    ]
    stores[0].start()
    stores[1].start()

    for g in range(4):
        arrive(ag.at[0, pl.ds(max(4 * g, 1), 4 if g else 3)], 18 + g)
        for m in (2, 1, 3):
            post(ag.at[0, pl.ds(4 * g, 4)], ag.at[m, pl.ds(4 * g, 4)], 22, at(dx=m))
    arrive(t4.at[pl.ds(1, NTG - 1)], 6)
    for p in range(NTG):
        rows, lanes = slice(p // 2 * 8, p // 2 * 8 + 8), slice(p % 2 * 128, p % 2 * 128 + 128)
        sgrad_ref[rows, lanes] = t4[(tgt - p + NTG) % NTG]
    stores[2].start()

    arrive(ag.at[pl.ds(1, 3)], 22)

    for c in range(COLS // 128):
        for h in range(2):
            o = 2 * c + h
            ox, oy, oz = o // NYZ, (o // NZ) % NY, o % NZ
            slot = ((y - oy + NY) % NY) * NZ + (z - oz + NZ) % NZ
            tgrad_ref[16 * h : 16 * h + 16, c * 128 : c * 128 + 128] = ag[(x - ox + NX) % NX, slot]
        if c % 8 == 7:
            lanes = pl.ds((c - 7) * 128, 1024)
            stores.append(pltpu.make_async_copy(tgrad_ref.at[:, lanes], tgrad_hbm.at[:, lanes], store.at[3 + c // 8]))
            stores[-1].start()

    def sent(ref, sem):
        pltpu.make_async_copy(ref, ref, send.at[sem]).wait()

    sent(t1r, 0)
    sent(a1r, 1)
    sent(a1q, 2)
    sent(qz, 3)
    sent(t2r, 4)
    sent(qr, 7)
    sent(qq, 23)
    sent(t4.at[pl.ds(1, NTG - 1)], 6)
    for g in range(4):
        sent(rxc.at[g], 8 + g)
        sent(rxv.at[g], 12 + g)
        sent(ag.at[0, pl.ds(max(4 * g, 1), 4 if g else 3)], 18 + g)
    sent(ryc, 16)
    sent(ryv, 17)
    sent(ag.at[pl.ds(1, 3)], 22)
    for c in stores:
        c.wait()


def deliver(*refs):
    sources, targets, held, sem_in, sem_out = refs[:4], refs[4:8], refs[8:12], refs[12], refs[13]
    parts = [(i, slice(None)) for i in range(3)] + [(3, pl.ds(8 * k, 8)) for k in range(4)]
    fetch = [pltpu.make_async_copy(sources[i].at[r], held[i].at[r], sem_in.at[n]) for n, (i, r) in enumerate(parts)]
    store = [pltpu.make_async_copy(held[i].at[r], targets[i].at[r], sem_out.at[n]) for n, (i, r) in enumerate(parts)]
    for c in fetch:
        c.start()
    for a, b in zip(fetch, store):
        a.wait()
        b.start()
    for c in store:
        c.wait()


def solution(mesh):
    def local(xs, xpot, xcot, ys, ypot, ycot):
        count = xs.shape[1] * mesh.shape["src"] * ys.shape[1] * mesh.shape["tgt"]
        hbm = pl.BlockSpec(memory_space=pltpu.HBM)
        results = (
            jax.ShapeDtypeStruct((1, ROWS), F32),
            jax.ShapeDtypeStruct((1, COLS), F32),
            jax.ShapeDtypeStruct((D, ROWS), F32),
            jax.ShapeDtypeStruct((D, COLS), F32),
        )
        outs = pl.pallas_call(
            functools.partial(kernel, -0.5 * math.log(count)),
            out_shape=results,
            in_specs=[hbm] * 6,
            out_specs=(hbm,) * 4,
            scratch_shapes=[
                pltpu.VMEM((D, ROWS), F32),
                pltpu.VMEM((1, ROWS), F32),
                pltpu.VMEM((1, ROWS), F32),
                pltpu.VMEM((D, COLS), F32),
                pltpu.VMEM((1, COLS), F32),
                pltpu.VMEM((1, COLS), F32),
                pltpu.VMEM((1, ROWS), F32),
                pltpu.VMEM((1, COLS), F32),
                pltpu.VMEM((D, ROWS), F32),
                pltpu.VMEM((D, COLS), F32),
                pltpu.VMEM((2, 224, CHUNK), BF16),
                pltpu.VMEM((ROWS, COLS), BF16),
                pltpu.VMEM((ROWS, COLS), BF16),
                pltpu.VMEM((1, COLS), F32),
                pltpu.VMEM((1, COLS), F32),
                pltpu.VMEM((64, COLS), F32),
                pltpu.VMEM((D, COLS), F32),
                pltpu.VMEM((D, COLS), F32),
                pltpu.VMEM((1, 2 * ROWS), F32),
                pltpu.VMEM((NTG - 1, 1, 2 * ROWS), F32),
                pltpu.VMEM((1, COLS), F32),
                pltpu.VMEM((NZ - 1, 1, COLS), F32),
                pltpu.VMEM((1, COLS), F32),
                pltpu.VMEM((NX * NY - 1, 1, COLS), F32),
                pltpu.VMEM((NX * NYZ, 16, 128), F32),
                pltpu.VMEM((NX * NYZ, 16, 128), F32),
                pltpu.VMEM((4, NX - 1, 4, 16, 128), F32),
                pltpu.VMEM((4, NX - 1, 4, 16, 128), F32),
                pltpu.VMEM((NYZ, 16, 128), F32),
                pltpu.VMEM((NYZ, 16, 128), F32),
                pltpu.VMEM((NYZ - 1, 16, 128), F32),
                pltpu.VMEM((NYZ - 1, 16, 128), F32),
                pltpu.VMEM((NTG, 2, 8, 128), F32),
                pltpu.VMEM((NTG - 1, 2, 8, 128), F32),
                pltpu.VMEM((NTG, 8, 128), F32),
                pltpu.VMEM((1, 512), F32),
                pltpu.VMEM((NTG - 1, 1, 512), F32),
                pltpu.VMEM((1, 512), F32),
                pltpu.VMEM((NX * NY - 1, 1, 512), F32),
                pltpu.VMEM((1, 512), F32),
                pltpu.VMEM((NZ - 1, 1, 512), F32),
                pltpu.VMEM((NX, NYZ, 16, 128), F32),
                pltpu.SemaphoreType.DMA((9,)),
                pltpu.SemaphoreType.DMA((7,)),
                pltpu.SemaphoreType.DMA((24,)),
                pltpu.SemaphoreType.DMA((24,)),
            ],
            compiler_params=pltpu.CompilerParams(
                collective_id=0, has_side_effects=True, vmem_limit_bytes=60 * 2**20
            ),
        )(xs, xpot.reshape(1, ROWS), xcot.reshape(1, ROWS), ys, ypot.reshape(1, COLS), ycot.reshape(1, COLS))
        sadj, tadj, sgrad, tgrad = pl.pallas_call(
            deliver,
            out_shape=results,
            in_specs=[hbm] * 4,
            out_specs=(hbm,) * 4,
            scratch_shapes=[pltpu.VMEM(r.shape, F32) for r in results]
            + [pltpu.SemaphoreType.DMA((7,)), pltpu.SemaphoreType.DMA((7,))],
            compiler_params=pltpu.CompilerParams(vmem_limit_bytes=60 * 2**20),
        )(*outs)
        return sadj.reshape(ROWS), tadj.reshape(COLS), sgrad, tgrad

    return jax.shard_map(
        local,
        mesh=mesh,
        in_specs=(P(None, "src"), P("src"), P("src"), P(None, "tgt"), P("tgt"), P("tgt")),
        out_specs=(P("src"), P("tgt"), P(None, "src"), P(None, "tgt")),
        check_vma=False,
    )
```

```python
import functools
import math

import jax
import jax.numpy as jnp
from jax import lax
from jax.experimental import pallas as pl
from jax.experimental.pallas import tpu as pltpu
from jax.sharding import PartitionSpec as P

MESH = pl.DeviceIdType.MESH
F32 = jnp.float32
BF16 = jnp.bfloat16

NX, NY, NZ, NTG = 4, 2, 8, 8
NYZ = NY * NZ

D = 32
ROWS = 256
COLS = 4096
XCOLS = COLS // NX
CHUNK = 512
RIDGE = 0.5


def split2(v):
    high = v.astype(BF16)
    return high, (v - high.astype(F32)).astype(BF16)


def split3(v):
    high = v.astype(BF16)
    rest = v - high.astype(F32)
    mid = rest.astype(BF16)
    return high, mid, (rest - mid.astype(F32)).astype(BF16)


def dot_nn(a, b):
    return lax.dot_general(a, b, (((1,), (0,)), ((), ())), preferred_element_type=F32)


def dot_nt(a, b):
    return lax.dot_general(a, b, (((1,), (1,)), ((), ())), preferred_element_type=F32)


def dot_tn(a, b):
    return lax.dot_general(a, b, (((0,), (0,)), ((), ())), preferred_element_type=F32)


def kernel(
    factor_log,
    xs_hbm, xpot_hbm, xcot_hbm, ys_hbm, ypot_hbm, ycot_hbm,
    sadj_hbm, tadj_hbm, sgrad_hbm, tgrad_hbm,
    xs_ref, xpot_ref, xcot_ref, ys_ref, ypot_ref, ycot_ref,
    sadj_ref, tadj_ref, sgrad_ref, tgrad_ref,
    bk, ph, pl_, cm_ref, pcs_ref, work, ubuf, wbuf,
    t1s, t1r, a1s, a1r, a1m, a1q,
    gc, gv, rxc, rxv, hc, hv, ryc, ryv,
    t2s, t2r, t4, qs, qr, qm, qq, qn, qz, ag,
    load, store, send, recv,
):
    loads = [
        pltpu.make_async_copy(a, b, load.at[i])
        for i, (a, b) in enumerate(
            [(xs_hbm, xs_ref), (xpot_hbm, xpot_ref), (xcot_hbm, xcot_ref),
             (ypot_hbm, ypot_ref), (ycot_hbm, ycot_ref)]
            + [(ys_hbm.at[:, pl.ds(k * 1024, 1024)], ys_ref.at[:, pl.ds(k * 1024, 1024)]) for k in range(4)]
        )
    ]
    for c in loads:
        c.start()
    src = lax.axis_index("src")
    tgt = lax.axis_index("tgt")
    x = src // NYZ
    y = (src // NZ) % NY
    z = src % NZ

    def at(dx=0, dy=0, dz=0, dt=0):
        there = ((x + dx) % NX) * NYZ + ((y + dy) % NY) * NZ + (z + dz) % NZ
        return (there, (tgt + dt) % NTG)

    def post(source, target, sem, peer):
        pltpu.make_async_remote_copy(
            src_ref=source, dst_ref=target, send_sem=send.at[sem], recv_sem=recv.at[sem],
            device_id=peer, device_id_type=MESH,
        ).start()

    def arrive(ref, sem):
        pltpu.make_async_copy(ref, ref, recv.at[sem]).wait()

    z_peers = [dict(dz=k) for k in (4, 3, 5, 2, 6, 1, 7)]
    xy_peers = [dict(dx=k // NY, dy=k % NY) for k in (5, 3, 7, 1, 4, 2, 6)]
    yz_peers = [dict(dy=k // NZ, dz=k % NZ) for k in range(1, NYZ)]
    x_peers = [dict(dx=k) for k in range(1, NX)]
    t_peers = [dict(dt=k) for k in (4, 3, 5, 2, 6, 1, 7)]

    barrier = pltpu.get_barrier_semaphore()
    greet = yz_peers + [p for p in xy_peers if p["dx"]] + t_peers
    for p in greet:
        pl.semaphore_signal(barrier, inc=1, device_id=at(**p), device_id_type=MESH)

    for c in loads[:5]:
        c.wait()
    xs = xs_ref[...]
    cs = xcot_ref[...]
    ct = ycot_ref[...]
    x1, x2, x3 = split3(xs * 4.0)
    row_term = (xpot_ref[...] - 2.0 * jnp.sum(xs * xs, axis=0, keepdims=True))
    r1, r2, r3 = split3(row_term)
    one_r = jnp.ones((1, ROWS), F32)
    tail_a = jnp.concatenate(
        [r1.astype(F32), r2.astype(F32), r3.astype(F32), one_r, one_r, one_r,
         jnp.zeros((26, ROWS), F32)], axis=0,
    ).astype(BF16)
    ak = jnp.concatenate([x1, x1, x2, x2, x1, x3, tail_a], axis=0)

    ones_crit = jnp.ones((1, ROWS), F32)
    cs_h, cs_l = split2(cs)
    s_crit = jnp.concatenate(
        [ones_crit, cs_h.astype(F32), cs_l.astype(F32), jnp.zeros((13, ROWS), F32)], axis=0
    ).astype(BF16)

    row_crit = jnp.zeros((16, ROWS), F32)
    one_c = jnp.ones((1, CHUNK), F32)
    for i in range(COLS // CHUNK):
        if i * CHUNK % 1024 == 0:
            loads[5 + i * CHUNK // 1024].wait()
        at_c = slice(i * CHUNK, i * CHUNK + CHUNK)
        yc = ys_ref[:, at_c]
        ctc = ycot_ref[:, at_c]
        y1, y2, y3 = split3(yc)
        col_term = (ypot_ref[:, at_c] - 2.0 * jnp.sum(yc * yc, axis=0, keepdims=True))
        c1, c2, c3 = split3(col_term + factor_log)
        tail_b = jnp.concatenate(
            [one_c, one_c, one_c, c1.astype(F32), c2.astype(F32), c3.astype(F32),
             jnp.zeros((26, CHUNK), F32)], axis=0,
        ).astype(BF16)
        bk[i % 2] = jnp.concatenate([y1, y2, y1, y2, y3, y1, tail_b], axis=0)
        plan = jnp.exp(dot_tn(ak, bk[i % 2]))
        high, low = split2(plan)
        ph[:, at_c] = high
        pl_[:, at_c] = low
        r = dot_nn(s_crit, high) + dot_nn(s_crit, low)
        cm_c = r[0:1]
        pcs_c = r[1:2] + r[2:3]
        cm_ref[:, at_c] = cm_c
        pcs_ref[:, at_c] = pcs_c
        a1s[:, at_c] = cm_c * ctc + pcs_c
        ct_h, ct_l = split2(ctc)
        t_crit = jnp.concatenate(
            [one_c, ct_h.astype(F32), ct_l.astype(F32), jnp.zeros((13, CHUNK), F32)], axis=0
        ).astype(BF16)
        row_crit = row_crit + dot_nt(t_crit, high) + dot_nt(t_crit, low)

    rm_part = row_crit[0:1]
    pct_part = row_crit[1:2] + row_crit[2:3]
    t1s[...] = jnp.concatenate([rm_part, pct_part], axis=1)

    pl.semaphore_wait(barrier, len(greet))

    for i, p in enumerate(z_peers):
        post(a1s, a1r.at[i], 1, at(**p))
    for i, p in enumerate(t_peers):
        post(t1s, t1r.at[i], 0, at(**p))

    def col_products(vectors, width):
        high, low = split2(vectors)
        stack = jnp.concatenate([high, low], axis=0)

        def step(i, c):
            at_c = pl.ds(pl.multiple_of(i * CHUNK, CHUNK), CHUNK)
            r = dot_nn(stack, ph[:, at_c]) + dot_nn(stack, pl_[:, at_c])
            work[0:width, at_c] = r[:width] + r[width:]
            return c

        lax.fori_loop(0, COLS // CHUNK, step, 0)

    def row_products(make, width):
        def step(i, acc):
            at_c = pl.ds(pl.multiple_of(i * CHUNK, CHUNK), CHUNK)
            high, low = split2(make(at_c))
            stack = jnp.concatenate([high, low], axis=0)
            r = dot_nt(stack, ph[:, at_c]) + dot_nt(stack, pl_[:, at_c])
            return acc + r[:width] + r[width:]

        return lax.fori_loop(0, COLS // CHUNK, step, jnp.zeros((width, ROWS), F32))

    def place(o):
        ox, oy, oz = o // NYZ, (o // NZ) % NY, o % NZ
        return ((ox - x + NX) % NX) * NYZ + ((oy - y + NY) % NY) * NZ + (oz - z + NZ) % NZ

    col_products(jnp.concatenate([xs, xs * cs], axis=0), 64)
    for c in range(COLS // 128):
        lanes = slice(c * 128, c * 128 + 128)
        yc = ys_ref[:, lanes]
        u = cm_ref[:, lanes] * yc - work[0:32, lanes]
        ubuf[:, lanes] = u
        g = ycot_ref[:, lanes] * u + pcs_ref[:, lanes] * yc - work[32:64, lanes]
        gc[place(2 * c)] = g[0:16]
        gc[place(2 * c + 1)] = g[16:32]

    def post_x(buf, into, base):
        for g in (3, 2, 1, 0):
            for m in (2, 1, 3):
                post(buf.at[pl.ds(m * NYZ + 4 * g, 4)], into.at[g, m - 1], base + g, at(dx=m))

    post_x(gc, rxc, 8)

    arrive(t1r, 0)
    rows_sum = t1s[...]
    for i in range(NTG - 1):
        rows_sum = rows_sum + t1r[i]
    rm = rows_sum[:, :ROWS]
    vs = rm * cs + rows_sum[:, ROWS:]
    col_products(jnp.concatenate([xs * vs, vs, jnp.zeros((15, ROWS), F32)], axis=0), 48)
    for c in range(COLS // 128):
        lanes = slice(c * 128, c * 128 + 128)
        wbuf[:, lanes] = work[32:33, lanes] * ys_ref[:, lanes] - work[0:32, lanes]


    def fold(v):
        acc = v[:, 0:128]
        for c in range(1, v.shape[1] // 128):
            acc = acc + v[:, c * 128 : c * 128 + 128]
        return acc

    arrive(a1r, 1)
    total = a1s[...]
    for i in range(NZ - 1):
        total = total + a1r[i]
    a1m[...] = total
    for i, p in enumerate(xy_peers):
        post(a1m, a1q.at[i], 2, at(**p))


    def make_c(at_c):
        yc = ys_ref[:, at_c]
        return jnp.concatenate([yc, yc * ycot_ref[:, at_c]], axis=0)

    rp = row_products(make_c, 64)
    row_u = rm_part * xs - rp[0:32]
    row_c = cs * row_u + pct_part * xs - rp[32:64]

    def add_x(buf, inbox, held, outbox, base, sem):
        for g in (3, 2, 1, 0):
            arrive(inbox.at[g], base + g)
            for s in range(4 * g, 4 * g + 4):
                held[s] = buf[s] + inbox[g, 0, s - 4 * g] + inbox[g, 1, s - 4 * g] + inbox[g, 2, s - 4 * g]
            for s in range(4 * g, 4 * g + 4):
                if s:
                    post(held.at[s], outbox.at[s - 1], sem, at(dy=s // NZ, dz=s % NZ))

    add_x(gc, rxc, hc, ryc, 8, 16)

    arrive(a1q, 2)
    vt = a1m[...]
    for i in range(NX * NY - 1):
        vt = vt + a1q[i]
    for c in range(COLS // 128):
        lanes = slice(c * 128, c * 128 + 128)
        g = vt[:, lanes] * ubuf[:, lanes] + wbuf[:, lanes]
        gv[place(2 * c)] = g[0:16]
        gv[place(2 * c + 1)] = g[16:32]
    post_x(gv, rxv, 12)
    tadj_ref[...] = vt

    of_src, of_tgt = 1.0 / NTG, 1.0 / (NX * NYZ)
    ct = ycot_ref[...]
    qs[...] = jnp.concatenate(
        [
            fold(cs * cs) * of_src + fold(ct * ct) * of_tgt,
            fold(cs * vs) * of_src + fold(ct * vt) * of_tgt,
            fold(vs * vs) * of_src + fold(vt * vt) * of_tgt,
            fold(rm_part * vs * vs) + fold(vt * (cm_ref[...] * vt + 2.0 * work[32:33, :])),
        ],
        axis=1,
    )
    for i, p in enumerate(t_peers):
        post(qs, qr.at[i], 7, at(**p))

    def make_v(at_c):
        v = tadj_ref[:, at_c]
        return jnp.concatenate([ys_ref[:, at_c] * v, v, jnp.zeros((15, CHUNK), F32)], axis=0)

    rp = row_products(make_v, 48)
    row_v = vs * row_u + rp[32:33] * xs - rp[0:32]
    for p in range(NTG):
        rows, lanes = slice(p // 2 * 8, p // 2 * 8 + 8), slice(p % 2 * 128, p % 2 * 128 + 128)
        slot = (p - tgt + NTG) % NTG
        t2s[slot, 0] = row_c[rows, lanes]
        t2s[slot, 1] = row_v[rows, lanes]
    for i, p in enumerate(t_peers):
        post(t2s.at[p["dt"]], t2r.at[i], 4, at(**p))

    arrive(qr, 7)
    inner = qs[...]
    for i in range(NTG - 1):
        inner = inner + qr[i]
    qm[...] = inner
    for i, p in enumerate(xy_peers):
        post(qm, qq.at[i], 23, at(**p))

    add_x(gv, rxv, hv, ryv, 12, 17)

    arrive(qq, 23)
    inner = qm[...]
    for i in range(NX * NY - 1):
        inner = inner + qq[i]
    qn[...] = inner
    for i, p in enumerate(z_peers):
        post(qn, qz.at[i], 3, at(**p))

    arrive(ryc, 16)
    piece_c = hc[0]
    for s in range(NYZ - 1):
        piece_c = piece_c + ryc[s]
    arrive(t2r, 4)
    row_piece = t2s[0]
    for i in range(NTG - 1):
        row_piece = row_piece + t2r[i]

    arrive(qz, 3)
    inner = qn[...]
    for i in range(NZ - 1):
        inner = inner + qz[i]
    m0, g1, g2, g3 = (
        jnp.sum(inner[:, q * 128 : q * 128 + 128], axis=1, keepdims=True) for q in range(4)
    )
    mu = g1 / m0
    h2 = jnp.maximum(g2 - g1 * mu, 0.0)
    h3 = g3 - 2.0 * mu * g2 + mu * mu * g1
    step0 = 1.0 / (RIDGE + mu)
    below = RIDGE * h2 + h3 - step0 * h2 * h2 / m0
    step1 = h2 / jnp.maximum(jnp.maximum(below, RIDGE * h2), 1e-37)
    beta = step0 * step0 * h2 / m0
    of_c = step0 + step1 * (beta + step0 * mu)
    of_v = -(step0 * step1)

    k_c = 4.0 * of_c
    k_v = 4.0 * of_v

    arrive(ryv, 17)
    piece_v = hv[0]
    for s in range(NYZ - 1):
        piece_v = piece_v + ryv[s]
    ag[0, 0] = k_c * piece_c + k_v * piece_v
    for s in (12, 11, 13, 10, 14, 9, 15, 8, 4, 3, 5, 2, 6, 1, 7):
        post(ag.at[0, 0], ag.at[0, s], 18 + s // 4, at(dy=s // NZ, dz=s % NZ))

    t4[0] = k_c * row_piece[0] + k_v * row_piece[1]
    for i, p in enumerate(t_peers):
        post(t4.at[0], t4.at[p["dt"]], 6, at(**p))
    sadj_ref[...] = of_c * cs + of_v * vs
    tadj_ref[...] = of_c * ct + of_v * vt
    stores = [
        pltpu.make_async_copy(sadj_ref, sadj_hbm, store.at[0]),
        pltpu.make_async_copy(tadj_ref, tadj_hbm, store.at[1]),
        pltpu.make_async_copy(sgrad_ref, sgrad_hbm, store.at[2]),
    ]
    stores[0].start()
    stores[1].start()

    for g in range(4):
        arrive(ag.at[0, pl.ds(max(4 * g, 1), 4 if g else 3)], 18 + g)
        for m in (2, 1, 3):
            post(ag.at[0, pl.ds(4 * g, 4)], ag.at[m, pl.ds(4 * g, 4)], 23 + m, at(dx=m))
    arrive(t4.at[pl.ds(1, NTG - 1)], 6)
    for p in range(NTG):
        rows, lanes = slice(p // 2 * 8, p // 2 * 8 + 8), slice(p % 2 * 128, p % 2 * 128 + 128)
        sgrad_ref[rows, lanes] = t4[(tgt - p + NTG) % NTG]
    stores[2].start()

    def put(m):
        ox = (x - m + NX) % NX
        for k in range(NYZ):
            slot = ((y - k // NZ + NY) % NY) * NZ + (z - k % NZ + NZ) % NZ
            lanes = pl.ds(pl.multiple_of(ox * XCOLS + k // 2 * 128, 128), 128)
            tgrad_ref[16 * (k % 2) : 16 * (k % 2) + 16, lanes] = ag[m, slot]
        lanes = pl.ds(pl.multiple_of(ox * XCOLS, XCOLS), XCOLS)
        stores.append(pltpu.make_async_copy(tgrad_ref.at[:, lanes], tgrad_hbm.at[:, lanes], store.at[3 + m]))
        stores[-1].start()

    put(0)
    for m in (1, 3, 2):
        arrive(ag.at[m], 23 + m)
        put(m)

    def sent(ref, sem):
        pltpu.make_async_copy(ref, ref, send.at[sem]).wait()

    sent(t1r, 0)
    sent(a1r, 1)
    sent(a1q, 2)
    sent(qz, 3)
    sent(t2r, 4)
    sent(qr, 7)
    sent(qq, 23)
    sent(t4.at[pl.ds(1, NTG - 1)], 6)
    for g in range(4):
        sent(rxc.at[g], 8 + g)
        sent(rxv.at[g], 12 + g)
        sent(ag.at[0, pl.ds(max(4 * g, 1), 4 if g else 3)], 18 + g)
    sent(ryc, 16)
    sent(ryv, 17)
    for m in range(1, NX):
        sent(ag.at[m], 23 + m)
    for c in stores:
        c.wait()


def deliver(*refs):
    sources, targets, held, sem_in, sem_out = refs[:4], refs[4:8], refs[8:12], refs[12], refs[13]
    parts = [(i, slice(None)) for i in range(3)] + [(3, pl.ds(8 * k, 8)) for k in range(4)]
    fetch = [pltpu.make_async_copy(sources[i].at[r], held[i].at[r], sem_in.at[n]) for n, (i, r) in enumerate(parts)]
    store = [pltpu.make_async_copy(held[i].at[r], targets[i].at[r], sem_out.at[n]) for n, (i, r) in enumerate(parts)]
    for c in fetch:
        c.start()
    for a, b in zip(fetch, store):
        a.wait()
        b.start()
    for c in store:
        c.wait()


def solution(mesh):
    def local(xs, xpot, xcot, ys, ypot, ycot):
        count = xs.shape[1] * mesh.shape["src"] * ys.shape[1] * mesh.shape["tgt"]
        hbm = pl.BlockSpec(memory_space=pltpu.HBM)
        results = (
            jax.ShapeDtypeStruct((1, ROWS), F32),
            jax.ShapeDtypeStruct((1, COLS), F32),
            jax.ShapeDtypeStruct((D, ROWS), F32),
            jax.ShapeDtypeStruct((D, COLS), F32),
        )
        outs = pl.pallas_call(
            functools.partial(kernel, -0.5 * math.log(count)),
            out_shape=results,
            in_specs=[hbm] * 6,
            out_specs=(hbm,) * 4,
            scratch_shapes=[
                pltpu.VMEM((D, ROWS), F32),
                pltpu.VMEM((1, ROWS), F32),
                pltpu.VMEM((1, ROWS), F32),
                pltpu.VMEM((D, COLS), F32),
                pltpu.VMEM((1, COLS), F32),
                pltpu.VMEM((1, COLS), F32),
                pltpu.VMEM((1, ROWS), F32),
                pltpu.VMEM((1, COLS), F32),
                pltpu.VMEM((D, ROWS), F32),
                pltpu.VMEM((D, COLS), F32),
                pltpu.VMEM((2, 224, CHUNK), BF16),
                pltpu.VMEM((ROWS, COLS), BF16),
                pltpu.VMEM((ROWS, COLS), BF16),
                pltpu.VMEM((1, COLS), F32),
                pltpu.VMEM((1, COLS), F32),
                pltpu.VMEM((64, COLS), F32),
                pltpu.VMEM((D, COLS), F32),
                pltpu.VMEM((D, COLS), F32),
                pltpu.VMEM((1, 2 * ROWS), F32),
                pltpu.VMEM((NTG - 1, 1, 2 * ROWS), F32),
                pltpu.VMEM((1, COLS), F32),
                pltpu.VMEM((NZ - 1, 1, COLS), F32),
                pltpu.VMEM((1, COLS), F32),
                pltpu.VMEM((NX * NY - 1, 1, COLS), F32),
                pltpu.VMEM((NX * NYZ, 16, 128), F32),
                pltpu.VMEM((NX * NYZ, 16, 128), F32),
                pltpu.VMEM((4, NX - 1, 4, 16, 128), F32),
                pltpu.VMEM((4, NX - 1, 4, 16, 128), F32),
                pltpu.VMEM((NYZ, 16, 128), F32),
                pltpu.VMEM((NYZ, 16, 128), F32),
                pltpu.VMEM((NYZ - 1, 16, 128), F32),
                pltpu.VMEM((NYZ - 1, 16, 128), F32),
                pltpu.VMEM((NTG, 2, 8, 128), F32),
                pltpu.VMEM((NTG - 1, 2, 8, 128), F32),
                pltpu.VMEM((NTG, 8, 128), F32),
                pltpu.VMEM((1, 512), F32),
                pltpu.VMEM((NTG - 1, 1, 512), F32),
                pltpu.VMEM((1, 512), F32),
                pltpu.VMEM((NX * NY - 1, 1, 512), F32),
                pltpu.VMEM((1, 512), F32),
                pltpu.VMEM((NZ - 1, 1, 512), F32),
                pltpu.VMEM((NX, NYZ, 16, 128), F32),
                pltpu.SemaphoreType.DMA((9,)),
                pltpu.SemaphoreType.DMA((7,)),
                pltpu.SemaphoreType.DMA((27,)),
                pltpu.SemaphoreType.DMA((27,)),
            ],
            compiler_params=pltpu.CompilerParams(
                collective_id=0, has_side_effects=True, vmem_limit_bytes=60 * 2**20
            ),
        )(xs, xpot.reshape(1, ROWS), xcot.reshape(1, ROWS), ys, ypot.reshape(1, COLS), ycot.reshape(1, COLS))
        sadj, tadj, sgrad, tgrad = pl.pallas_call(
            deliver,
            out_shape=results,
            in_specs=[hbm] * 4,
            out_specs=(hbm,) * 4,
            scratch_shapes=[pltpu.VMEM(r.shape, F32) for r in results]
            + [pltpu.SemaphoreType.DMA((7,)), pltpu.SemaphoreType.DMA((7,))],
            compiler_params=pltpu.CompilerParams(vmem_limit_bytes=60 * 2**20),
        )(*outs)
        return sadj.reshape(ROWS), tadj.reshape(COLS), sgrad, tgrad

    return jax.shard_map(
        local,
        mesh=mesh,
        in_specs=(P(None, "src"), P("src"), P("src"), P(None, "tgt"), P("tgt"), P("tgt")),
        out_specs=(P("src"), P("tgt"), P(None, "src"), P(None, "tgt")),
        check_vma=False,
    )
```
